256 devices in a mesh: section: 4 (over y), dp: 64 (over x, z, core).
Axes of the slice: x: 4, y: 4, z: 8, core: 2. Of those that a mesh axis runs over, the one named last changes fastest.
Arguments:
- hidden: bfloat16 [4, 8192, 8192], P('section', 'dp'), may hold values from -6 to 6
- cotangent: bfloat16 [8192, 8192], P('dp'), may hold values from -6 to 6
- w_value: bfloat16 [4, 8192, 512], P('section', 'dp'), may hold values from -0.0625 to 0.0625
- w_out_t: bfloat16 [4, 8192, 512], P('section', 'dp'), may hold values from -0.0625 to 0.0625
- p_in: bfloat16 [4, 8192, 64], P('section'), may hold values from -0.015625 to 0.015625
- p_value_out: bfloat16 [4, 512, 64], P('section'), may hold values from -0.0625 to 0.0625
- p_value_in: bfloat16 [4, 512, 64], P('section'), may hold values from -0.0625 to 0.0625
- p_out: bfloat16 [4, 8192, 64], P('section'), may hold values from -0.015625 to 0.015625
- segments: int32 [8192], P('dp'), may hold values from 0 to 63, never falling along the last dimension, each value on 1 to 1024 neighbouring positions
- owner_slot: int32 [64], replicated, may hold values from 0 to 63, each once
Outputs:
- doc_grads: float32 [4, 2, 64, 4096], P('section', None, 'dp')
The draws below stay inside these ranges and needn't reach their ends.
Inputs may be any that keep to these rules, and one draw needn't show every extreme that they name: `segments`: document numbers never fall along the row; each document has 1 to 1024 tokens and one has exactly 1024. `owner_slot`: each slot is taken by exactly one document.
All inputs are finite; a program needn't handle non-finite values.
Results may differ from the reference program's by a relative error of at most 0.008.
Values may be sent and summed in bfloat16 or wider, within the bound.
No kernel may reach another device: no remote copies, remote signals or barrier semaphores. Data moves between devices by JAX's collectives and lax.ppermute only.
A program may use at most 128 MiB of HBM per device.

```python
import math
import jax
import jax.numpy as jnp
import numpy as np
from jax import lax

D = 8192
KV = 512
R = 64
TOK_DEV = 128
SECTIONS = 4
LENGTH = 8192
DOCS = 64
MOST = 1024


def steps_of(key, shape, cuts, low, high):
    loudness, own = 1.0, jax.random.fold_in(key, 6)
    for axis_at, shards_of in cuts:
        draws = jnp.exp(jax.random.uniform(jax.random.fold_in(own, axis_at), (shards_of,), jnp.float32, low / len(cuts), high / len(cuts)))
        loudness = loudness * jnp.repeat(draws, shape[axis_at] // shards_of).reshape([-1 if axis == axis_at else 1 for axis in range(len(shape))])
    return loudness


def length_profile(count, total, most, slope):
    portions = [(1 << 20) // math.isqrt(rank ** slope) + 1 for rank in range(2, count + 1)]
    spare, counts = total - most - (count - 1), [1] * (count - 1)
    while spare > 0:
        free = [i for i in range(count - 1) if counts[i] < most]
        mass, budget = sum([portions[i] for i in free]), spare
        for i in free:
            addition = min(most - counts[i], max(1, budget * portions[i] // mass), spare)
            counts[i] = counts[i] + addition
            spare = spare - addition
    return np.array([most] + counts)


def uneven_parts(own_key, amount, total, limit, slope):
    if amount == 2:
        one = jax.random.randint(own_key, (), max(1, total - limit), min(limit, total - 1) + 1)
        return jnp.stack([one, total - one])
    lengths = jnp.asarray(length_profile(amount, total, limit, slope), jnp.int32)
    twos = (amount - 1) // 2
    source_of, sink = lengths[1:1 + 2 * twos:2], lengths[2:2 + 2 * twos:2]
    room = jnp.minimum(source_of - 1, limit - sink)
    passed = jax.random.randint(jax.random.fold_in(own_key, 1), (twos,), 0, 1 << 20) % (room + 1)
    lengths = lengths.at[1:1 + 2 * twos:2].set(source_of - passed).at[2:2 + 2 * twos:2].set(sink + passed)
    return lengths[jax.random.permutation(jax.random.fold_in(own_key, 2), amount)]


def gaussian(stream_key, extent, scale, limit, cuts=(), kind=jnp.bfloat16):
    result = jax.random.normal(stream_key, extent, jnp.float32) * scale
    if len(cuts) > 0:
        result = steps_of(stream_key, extent, cuts, -0.22, 0.18) * result
    return jnp.clip(result, min=-limit, max=limit).astype(kind)


def setup_inputs(seed: int = 0) -> dict:
    seeds = jax.random.split(jax.random.key(seed), 11)
    return {
        "hidden": gaussian(seeds[0], (SECTIONS, LENGTH, D), 1.0, 6.0, ((0, 4), (1, 64))),
        "cotangent": gaussian(seeds[1], (LENGTH, D), 1.0, 6.0, ((0, 64),)),
        "w_value": gaussian(seeds[2], (SECTIONS, D, KV), D ** -0.5, 0.0625, ((0, 4), (1, 64))),
        "w_out_t": gaussian(seeds[3], (SECTIONS, D, KV), D ** -0.5, 0.0625, ((0, 4), (1, 64))),
        "p_in": gaussian(seeds[4], (SECTIONS, D, R), (16 * D) ** -0.5, 0.015625, ((0, 4),)),
        "p_value_out": gaussian(seeds[5], (SECTIONS, KV, R), (16 * KV) ** -0.5, 0.0625, ((0, 4),)),
        "p_value_in": gaussian(seeds[6], (SECTIONS, KV, R), (16 * KV) ** -0.5, 0.0625, ((0, 4),)),
        "p_out": gaussian(seeds[7], (SECTIONS, D, R), (16 * D) ** -0.5, 0.015625, ((0, 4),)),
        "segments": jnp.searchsorted(jnp.cumsum(uneven_parts(seeds[8], DOCS, LENGTH, MOST, 2)), jnp.arange(LENGTH), side="right").astype(jnp.int32),
        "owner_slot": jax.random.permutation(seeds[9], DOCS).astype(jnp.int32),
    }


def doc_table(packed, slots):
    rank = packed.shape[1] // 4
    blocks = packed.reshape(LENGTH // TOK_DEV, TOK_DEV, 4 * rank)
    slot_blocks = slots.reshape(LENGTH // TOK_DEV, TOK_DEV)

    def step(carry, item):
        rows, slot_row = item
        onehot = (slot_row[:, None] == jnp.arange(DOCS, dtype=jnp.int32)[None, :]).astype(jnp.bfloat16)
        tables = []
        for layer in range(2):
            left = rows[:, 2 * layer * rank:(2 * layer + 1) * rank]
            right = rows[:, (2 * layer + 1) * rank:(2 * layer + 2) * rank]
            spread = (onehot[:, :, None] * left[:, None, :]).reshape(TOK_DEV, DOCS * rank)
            table = lax.dot_general(spread, right, (((0,), (0,)), ((), ())), preferred_element_type=jnp.float32)
            tables.append(table.reshape(DOCS, rank * rank))
        return carry + jnp.stack(tables), None

    init = jnp.zeros((2, DOCS, rank * rank), jnp.float32)
    total, unused = lax.scan(step, init, (blocks, slot_blocks))
    return total


def reference(hidden, cotangent, w_value, w_out_t, p_in, p_value_out, p_value_in, p_out, segments, owner_slot):
    slots = owner_slot[segments].astype(jnp.int32)
    grad = cotangent
    tables = [None] * SECTIONS
    for section in reversed(range(SECTIONS)):
        acts = hidden[section]
        upd = jnp.dot(grad, w_out_t[section], preferred_element_type=jnp.float32).astype(jnp.bfloat16)
        value = jnp.dot(acts, w_value[section], preferred_element_type=jnp.float32).astype(jnp.bfloat16)
        first_in = jnp.dot(acts, p_in[section], preferred_element_type=jnp.float32).astype(jnp.bfloat16)
        first_out = jnp.dot(upd, p_value_out[section], preferred_element_type=jnp.float32).astype(jnp.bfloat16)
        second_in = jnp.dot(value, p_value_in[section], preferred_element_type=jnp.float32).astype(jnp.bfloat16)
        second_out = jnp.dot(grad, p_out[section], preferred_element_type=jnp.float32).astype(jnp.bfloat16)
        packed = jnp.concatenate([first_in, first_out, second_in, second_out], axis=1)
        tables[section] = doc_table(packed, slots)
        back = jnp.dot(upd, w_value[section].T, preferred_element_type=jnp.float32)
        grad = (grad.astype(jnp.float32) + back).astype(jnp.bfloat16)
    return jnp.stack(tables)
```

```python
import jax
import jax.numpy as jnp
from jax import lax
from jax.sharding import Mesh, PartitionSpec as P

XZ = ("x", "z")
DP = ("x", "z", "c")
SWAP = [(0, 1), (1, 0)]
BF16 = jnp.bfloat16
F32 = jnp.float32


def dot(left, right, left_dim=1):
    return lax.dot_general(
        left, right, (((left_dim,), (0,)), ((), ())), preferred_element_type=F32
    )


def from_above(value, steps):
    count = lax.axis_size("y")
    return lax.ppermute(value, "y", [(i, i - steps) for i in range(steps, count)])


def halves(mine, core, axis):
    got = lax.ppermute(mine, "c", SWAP)
    first = jnp.where(core == 0, mine, got)
    second = jnp.where(core == 0, got, mine)
    return jnp.concatenate([first, second], axis=axis)


def grams(wv, right, core):
    width = wv.shape[1] // 2
    mine = lax.dynamic_slice_in_dim(wv, core * width, width, 1)
    other = lax.dynamic_slice_in_dim(wv, (1 - core) * width, width, 1)
    left = jnp.concatenate([mine, lax.ppermute(other, "c", SWAP)], axis=0)
    rows = jnp.concatenate([right, lax.ppermute(right, "c", SWAP)], axis=0)
    parts = [dot(from_above(left, k), rows, 0).astype(BF16) for k in (1, 2, 3)]
    ranks = lax.axis_size(XZ)
    own = jnp.concatenate(parts, axis=0).reshape(ranks, -1, right.shape[1])
    slices = lax.all_to_all(own, XZ, 0, 0)
    total = jnp.sum(slices.astype(F32), axis=0).astype(BF16)
    every = lax.all_to_all(jnp.broadcast_to(total[None], own.shape), XZ, 0, 0)
    return every.reshape(3, width, right.shape[1])


def solve(half, pv_out, core, kv):
    above_one = from_above(half[:2, :, :kv], 1)
    above_two = from_above(half[:1, :, :kv], 2)
    own = halves(half, core, 1)
    g_one = halves(above_one, core, 1)
    g_two = halves(above_two, core, 1)
    first = [
        jnp.concatenate([dot(own[k, :, :kv], pv_out), own[k, :, kv:].astype(F32)], axis=1)
        for k in range(3)
    ]
    e_one = first[0].astype(BF16)
    e_two = (first[1] + dot(g_one[0], e_one)).astype(BF16)
    e_three = (first[2] + dot(g_one[1], e_one) + dot(g_two[0], e_two)).astype(BF16)
    return jnp.concatenate([e_one, e_two, e_three], axis=0)


def doc_sums(left, right, slots, core, rank):
    owners = lax.axis_size(XZ)
    named = 2 * jnp.arange(owners, dtype=jnp.int32) + core
    onehot = (slots[:, None] == named[None, :]).astype(BF16)
    spread = (onehot[:, :, None] * left[:, None, :]).reshape(left.shape[0], owners * 2 * rank)
    table = dot(spread, right, 0).reshape(owners, 2 * rank, 2 * rank)
    lane = lax.broadcasted_iota(jnp.int32, (1, rank, 2 * rank), 2)
    return jnp.where(lane < rank, table[:, :rank], table[:, rank:]).astype(BF16)


def body(
    hidden, cotangent, w_value, w_out_t, p_in, p_value_out, p_value_in, p_out, segments, owner_slot
):
    core = lax.axis_index("c")
    device = lax.axis_index(DP)
    wv, wo, acts = w_value[0], w_out_t[0], hidden[0]
    rows, kv = wv.shape
    rank = p_in.shape[2]
    documents = owner_slot.shape[0]

    mixed = jnp.concatenate([wo, dot(wv, p_value_in[0]).astype(BF16)], axis=1)
    full = lax.all_gather(mixed, DP, axis=0, tiled=True)

    out_rows = lax.dynamic_slice_in_dim(p_out[0], device * rows, rows, 0)
    half = grams(wv, jnp.concatenate([wo, out_rows], axis=1), core)
    spread_e = solve(half, p_value_out[0], core, kv)

    match = segments[:, None] == jnp.arange(documents, dtype=jnp.int32)[None, :]
    slots = jnp.sum(jnp.where(match, owner_slot[None, :], 0), axis=1)
    slots = jnp.concatenate([slots, lax.ppermute(slots, "c", SWAP)])
    first_in = dot(acts, p_in[0])
    direct_out = dot(cotangent, p_out[0])
    tokens = cotangent.shape[0]
    both = jnp.concatenate([cotangent, acts], axis=0)

    product = dot(both, full).astype(BF16)
    upd = product[:tokens, :kv]
    above = jnp.concatenate([from_above(upd, k) for k in (1, 2, 3)], axis=1)
    direct = jnp.concatenate([dot(upd, p_value_out[0]), direct_out], axis=1)
    right = (direct + dot(above, spread_e)).astype(BF16)
    left = jnp.concatenate([first_in.astype(BF16), product[tokens:, kv:]], axis=1)
    packed = jnp.concatenate([left, right], axis=1)
    packed = jnp.concatenate([packed, lax.ppermute(packed, "c", SWAP)], axis=0)
    sums = doc_sums(packed[:, : 2 * rank], packed[:, 2 * rank :], slots, core, rank)
    parts = lax.all_to_all(sums, XZ, 0, 0)
    total = jnp.sum(parts.astype(F32), axis=0)
    tables = total.reshape(rank, 2, rank).transpose(1, 0, 2)
    return tables.reshape(1, 2, 1, rank * rank)


def solution(mesh):
    grid = Mesh(mesh.devices.reshape(4, 4, 8, 2), ("y", "x", "z", "c"))
    placed = (
        P("y", DP, None),
        P(DP, None),
        P("y", DP, None),
        P("y", DP, None),
        P("y", None, None),
        P("y", None, None),
        P("y", None, None),
        P("y", None, None),
        P(DP),
        P(),
    )
    return jax.shard_map(
        body, mesh=grid, in_specs=placed, out_specs=P("y", None, DP, None), check_vma=False
    )
```

```python
import jax
import jax.numpy as jnp
from jax import lax
from jax.sharding import Mesh, PartitionSpec as P

XZ = ("x", "z")
DP = ("x", "z", "c")
SWAP = [(0, 1), (1, 0)]
BF16 = jnp.bfloat16
F32 = jnp.float32


def dot(left, right, left_dim=1):
    return lax.dot_general(
        left, right, (((left_dim,), (0,)), ((), ())), preferred_element_type=F32
    )


def send(value, pairs):
    return lax.ppermute(value, "y", pairs)


def grams(wv, right, plane, core):
    width = wv.shape[1] // 2
    mine = lax.dynamic_slice_in_dim(wv, core * width, width, 1)
    other = lax.dynamic_slice_in_dim(wv, (1 - core) * width, width, 1)
    left = jnp.concatenate([mine, lax.ppermute(other, "c", SWAP)], axis=0)
    rows = jnp.concatenate([right, lax.ppermute(right, "c", SWAP)], axis=0)
    near = send(left, [(1, 0), (2, 1), (3, 2)])
    far = send(rows, [(1, 3)])
    two, three = send(left, [(2, 0)]), send(left, [(3, 0)])
    kv, columns = wv.shape[1], right.shape[1]
    main = dot(jnp.where(plane == 3, left, near), jnp.where(plane == 3, far, rows), 0)
    own = [dot(item, rows[:, kv:], 0) for item in (near, two, three)]
    own = jnp.concatenate(own + [jnp.zeros((width, columns - 3 * (columns - kv)), F32)], axis=1)
    parts = jnp.where(plane == 0, own, main).astype(BF16)
    ranks = lax.axis_size(XZ)
    shape = (ranks, width // ranks, columns)
    slices = lax.all_to_all(parts.reshape(shape), XZ, 0, 0)
    total = jnp.sum(slices.astype(F32), axis=0).astype(BF16)
    every = lax.all_to_all(jnp.broadcast_to(total[None], shape), XZ, 0, 0)
    return every.reshape(width, columns)


def solve(half, plane, core, kv):
    count = lax.axis_size("y")
    around = [half] + [
        send(half, [(i, (i - k) % count) for i in range(count)]) for k in range(1, count)
    ]
    planes = []
    for p in range(count):
        steps = (p - plane) % count
        item = around[0]
        for k in range(1, count):
            item = jnp.where(steps == k, around[k], item)
        planes.append(item)
    mine = jnp.stack(planes)
    got = lax.ppermute(mine, "c", SWAP)
    first, second = jnp.where(core == 0, mine, got), jnp.where(core == 0, got, mine)
    table = jnp.concatenate([first, second], axis=1)
    block = half.shape[1] - kv
    f01, f02, f03 = (table[0, :, k * block : (k + 1) * block] for k in range(3))
    g21, g32, g31 = (table[k, :, :kv] for k in (1, 2, 3))
    f12, f23, f13 = (table[k, :, kv:] for k in (1, 2, 3))
    e02 = (f02.astype(F32) + dot(g21, f01)).astype(BF16)
    e13 = (f13.astype(F32) + dot(g32, f12)).astype(BF16)
    e03 = (f03.astype(F32) + dot(g31, f01) + dot(g32, e02)).astype(BF16)
    zero = jnp.zeros_like(f01)
    columns = (
        jnp.where(plane == 1, f01, jnp.where(plane == 2, e02, e03)),
        jnp.where(plane == 2, f12, jnp.where(plane == 3, e13, zero)),
        jnp.where(plane == 3, f23, zero),
    )
    return jnp.concatenate(columns, axis=1)


def doc_sums(left, right, slots, core, rank):
    owners = lax.axis_size(XZ)
    named = 2 * jnp.arange(owners, dtype=jnp.int32) + core
    onehot = (slots[:, None] == named[None, :]).astype(BF16)
    spread = (onehot[:, :, None] * left[:, None, :]).reshape(left.shape[0], owners * 2 * rank)
    table = dot(spread, right, 0).reshape(owners, 2 * rank, 2 * rank)
    lane = lax.broadcasted_iota(jnp.int32, (1, rank, 2 * rank), 2)
    return jnp.where(lane < rank, table[:, :rank], table[:, rank:]).astype(BF16)


def body(
    hidden, cotangent, w_value, w_out_t, p_in, p_value_out, p_value_in, p_out, segments, owner_slot
):
    plane, core = lax.axis_index("y"), lax.axis_index("c")
    device = lax.axis_index(DP)
    wv, wo, acts = w_value[0], w_out_t[0], hidden[0]
    rows, kv = wv.shape
    rank = p_in.shape[2]
    documents = owner_slot.shape[0]

    mixed = jnp.concatenate([wo, dot(wv, p_value_in[0]).astype(BF16)], axis=1)
    full = lax.all_gather(mixed, DP, axis=0, tiled=True)

    out_rows = lax.dynamic_slice_in_dim(p_out[0], device * rows, rows, 0)
    projected = dot(wo, p_value_out[0]).astype(BF16)
    right_rows = jnp.concatenate([wo, projected, out_rows], axis=1)
    spread_e = solve(grams(wv, right_rows, plane, core), plane, core, kv)

    match = segments[:, None] == jnp.arange(documents, dtype=jnp.int32)[None, :]
    slots = jnp.sum(jnp.where(match, owner_slot[None, :], 0), axis=1)
    slots = jnp.concatenate([slots, lax.ppermute(slots, "c", SWAP)])
    first_in = dot(acts, p_in[0])
    direct_out = dot(cotangent, p_out[0])
    tokens = cotangent.shape[0]
    both = jnp.concatenate([cotangent, acts], axis=0)

    product = dot(both, full).astype(BF16)
    upd = product[:tokens, :kv]
    right = jnp.concatenate([dot(upd, p_value_out[0]), direct_out], axis=1)
    below = dot(upd, spread_e).astype(BF16)
    count = lax.axis_size("y")
    for k in range(1, count):
        start = jnp.maximum(plane - k, 0) * 2 * rank
        item = lax.dynamic_slice_in_dim(below, start, 2 * rank, 1)
        right = right + send(item, [(i, i - k) for i in range(k, count)]).astype(F32)
    right = right.astype(BF16)
    left = jnp.concatenate([first_in.astype(BF16), product[tokens:, kv:]], axis=1)
    packed = jnp.concatenate([left, right], axis=1)
    packed = jnp.concatenate([packed, lax.ppermute(packed, "c", SWAP)], axis=0)
    sums = doc_sums(packed[:, : 2 * rank], packed[:, 2 * rank :], slots, core, rank)
    parts = lax.all_to_all(sums, XZ, 0, 0)
    total = jnp.sum(parts.astype(F32), axis=0)
    tables = total.reshape(rank, 2, rank).transpose(1, 0, 2)
    return tables.reshape(1, 2, 1, rank * rank)


def solution(mesh):
    grid = Mesh(mesh.devices.reshape(4, 4, 8, 2), ("y", "x", "z", "c"))
    placed = (
        P("y", DP, None),
        P(DP, None),
        P("y", DP, None),
        P("y", DP, None),
        P("y", None, None),
        P("y", None, None),
        P("y", None, None),
        P("y", None, None),
        P(DP),
        P(),
    )
    return jax.shard_map(
        body, mesh=grid, in_specs=placed, out_specs=P("y", None, DP, None), check_vma=False
    )
```

```python
import jax
import jax.numpy as jnp
from jax import lax
from jax.experimental import pallas as pl
from jax.experimental.pallas import tpu as pltpu
from jax.sharding import Mesh, PartitionSpec as P

XZ = ("x", "z")
DP = ("x", "z", "c")
SWAP = [(0, 1), (1, 0)]
BF16 = jnp.bfloat16
F32 = jnp.float32


def dot(left, right, left_dim=1):
    return lax.dot_general(
        left, right, (((left_dim,), (0,)), ((), ())), preferred_element_type=F32
    )


def send(value, pairs):
    return lax.ppermute(value, "y", pairs)


def swap(value):
    return lax.ppermute(value, "c", SWAP)


def half_of(value, core, axis=1):
    width = value.shape[axis] // 2
    return lax.dynamic_slice_in_dim(value, core * width, width, axis)


def ordered(mine, core):
    got = swap(mine)
    return jnp.concatenate([jnp.where(core == 0, mine, got), jnp.where(core == 0, got, mine)])


def gather(wo, projected, core):
    mine = jnp.concatenate([half_of(wo, core), projected], axis=1)
    other = jnp.concatenate([half_of(wo, 1 - core), projected], axis=1)
    got = swap(other)
    chip = jnp.concatenate([jnp.where(core == 0, mine, got), jnp.where(core == 0, got, mine)])
    width = wo.shape[1] // 2
    shard = jnp.concatenate([chip[:, :width], chip[:, width:].T], axis=0)
    count, place = lax.axis_size("x"), lax.axis_index("x")
    around = [shard] + [
        lax.ppermute(shard, "x", [(i, (i - k) % count) for i in range(count)])
        for k in range(1, count)
    ]
    column = []
    for p in range(count):
        steps = (p - place) % count
        item = around[0]
        for k in range(1, count):
            item = jnp.where(steps == k, around[k], item)
        column.append(item)
    return lax.all_gather(jnp.stack(column), "z", axis=0, tiled=True)


def product_kernel(across, cot_mine, cot_got, act_mine, act_got, block, upd, value, upd_sum, value_sum):
    step, last = pl.program_id(0), pl.num_programs(0) - 1
    width = block.shape[2]

    @pl.when(step == 0)
    def _():
        upd_sum[...] = jnp.zeros_like(upd_sum)
        value_sum[...] = jnp.zeros_like(value_sum)

    for k in range(across):
        start = pl.multiple_of((k * (last + 1) + step) * width, width)
        cols = pl.ds(start, width)
        cot = jnp.concatenate([cot_mine[:, cols], cot_got[:, cols]], axis=0)
        act = jnp.concatenate([act_mine[:, cols], act_got[:, cols]], axis=0)
        upd_sum[...] += jnp.dot(cot, block[k, :width, :], preferred_element_type=F32)
        value_sum[...] += lax.dot_general(
            act, block[k, width:, :], (((1,), (1,)), ((), ())), preferred_element_type=F32
        )

    @pl.when(step == last)
    def _():
        upd[...] = upd_sum[...].astype(BF16)
        value[...] = value_sum[...].astype(BF16)


def products(cot_mine, cot_got, act_mine, act_got, full, across):
    tokens, depth = cot_mine.shape
    count, rows, width = full.shape
    rank = rows - width
    whole = pl.BlockSpec(memory_space=pltpu.VMEM)
    return pl.pallas_call(
        lambda *refs: product_kernel(across, *refs),
        grid=(count // across,),
        in_specs=[whole] * 4 + [pl.BlockSpec((across, rows, width), lambda i: (i, 0, 0))],
        out_specs=[whole, whole],
        out_shape=[
            jax.ShapeDtypeStruct((2 * tokens, width), BF16),
            jax.ShapeDtypeStruct((2 * tokens, rank), BF16),
        ],
        scratch_shapes=[
            pltpu.VMEM((2 * tokens, width), F32),
            pltpu.VMEM((2 * tokens, rank), F32),
        ],
        compiler_params=pltpu.CompilerParams(
            dimension_semantics=("arbitrary",), vmem_limit_bytes=40 * 1024 * 1024
        ),
        cost_estimate=pl.CostEstimate(
            flops=4 * tokens * depth * rows, bytes_accessed=2 * full.size, transcendentals=0
        ),
    )(cot_mine, cot_got, act_mine, act_got, full)


def grams(wv, right, plane, core, later):
    kv, columns = wv.shape[1], right.shape[1]
    width = kv // 2
    near, far = send(wv, [(3, 0), (2, 1)]), send(wv, [(3, 1)])
    above, below = send(right, [(0, 1), (1, 2), (2, 3)]), send(right, [(1, 0)])
    right = jnp.where(plane == 0, below, above)
    lefts = [jnp.where(plane == 0, near, wv), near, far]
    got = swap(jnp.concatenate([half_of(item, 1 - core) for item in lefts], axis=1))
    mine = jnp.concatenate([half_of(item, core) for item in lefts], axis=1)
    left = jnp.concatenate([mine, got], axis=0)
    rows = jnp.concatenate([right, swap(right)], axis=0)
    main = dot(left[:, :width], rows, 0)
    own = [dot(left[:, k * width : (k + 1) * width], rows[:, kv:], 0) for k in range(3)]
    own = jnp.concatenate(own + [jnp.zeros((width, columns - 3 * (columns - kv)), F32)], axis=1)
    parts = jnp.where(plane == 1, own, main).astype(BF16)
    parts, *later = lax.optimization_barrier((parts, *later))
    ranks = lax.axis_size(XZ)
    shape = (ranks, width // ranks, columns)
    slices = lax.all_to_all(parts.reshape(shape), XZ, 0, 0)
    total = jnp.sum(slices.astype(F32), axis=0).astype(BF16)
    every = lax.all_to_all(jnp.broadcast_to(total[None], shape), XZ, 0, 0)
    return every.reshape(width, columns), [swap(item) for item in later]


def solve(half, plane, core, kv):
    block = half.shape[1] - kv
    above = send(half, [(1, 2), (2, 3)])
    wrap = send(half, [(0, 3)])
    twice = send(half[:, : 3 * block], [(1, 3)])
    first = jnp.where(plane == 1, half[:, : 3 * block], above[:, : 3 * block])
    first = jnp.where(plane == 3, twice, first)
    second = jnp.where(plane == 2, half, above)
    f01, f02, f03 = (first[:, k * block : (k + 1) * block] for k in range(3))
    g21, g31, g32 = second[:, :kv], wrap[:, :kv], half[:, :kv]
    f12, f13, f23 = second[:, kv:], wrap[:, kv:], half[:, kv:]
    known = ordered(jnp.concatenate([f01, f12], axis=1), core)
    f01_all, f12_all = known[:, :block], known[:, block:]
    e02 = (f02.astype(F32) + dot(g21, f01_all)).astype(BF16)
    e02_all = ordered(e02, core)
    e13 = (f13.astype(F32) + dot(g32, f12_all)).astype(BF16)
    e03 = (f03.astype(F32) + dot(g31, f01_all) + dot(g32, e02_all)).astype(BF16)
    zero = jnp.zeros_like(f01)
    columns = (
        jnp.where(plane == 1, f01, jnp.where(plane == 2, e02, e03)),
        jnp.where(plane == 2, f12, jnp.where(plane == 3, e13, zero)),
        jnp.where(plane == 3, f23, zero),
    )
    return jnp.concatenate(columns, axis=1)


def doc_sums(left, right, slots, core, rank):
    owners = lax.axis_size(XZ)
    named = 2 * jnp.arange(owners, dtype=jnp.int32) + core
    onehot = (slots[:, None] == named[None, :]).astype(BF16)
    spread = (onehot[:, :, None] * left[:, None, :]).reshape(left.shape[0], owners * 2 * rank)
    table = dot(spread, right, 0).reshape(owners, 2 * rank, 2 * rank)
    lane = lax.broadcasted_iota(jnp.int32, (1, rank, 2 * rank), 2)
    return jnp.where(lane < rank, table[:, :rank], table[:, rank:]).astype(BF16)


def body(
    hidden, cotangent, w_value, w_out_t, p_in, p_value_out, p_value_in, p_out, segments, owner_slot
):
    plane, core = lax.axis_index("y"), lax.axis_index("c")
    device = lax.axis_index(DP)
    wv, wo, acts = w_value[0], w_out_t[0], hidden[0]
    rows, kv = wv.shape
    rank = p_in.shape[2]
    documents = owner_slot.shape[0]
    tokens = cotangent.shape[0]

    full = gather(wo, dot(wv, p_value_in[0]).astype(BF16), core)

    out_rows = lax.dynamic_slice_in_dim(p_out[0], device * rows, rows, 0)
    right_rows = jnp.concatenate([wo, dot(wo, p_value_out[0]).astype(BF16), out_rows], axis=1)
    half, (cot_got, act_got) = grams(wv, right_rows, plane, core, (cotangent, acts))
    spread_e = solve(half, plane, core, kv)

    match = segments[:, None] == jnp.arange(documents, dtype=jnp.int32)[None, :]
    slots = jnp.sum(jnp.where(match, owner_slot[None, :], 0), axis=1)
    slots = jnp.concatenate([slots, swap(slots)])
    first_in = dot(acts, p_in[0]).astype(BF16)
    first_in = jnp.concatenate([first_in, swap(first_in)], axis=0)
    direct_out = dot(cotangent, p_out[0])
    direct_out = jnp.concatenate([direct_out, jnp.zeros_like(direct_out)], axis=0)

    upd, second_in = products(
        cotangent, cot_got, acts, act_got, full.reshape(-1, *full.shape[-2:]), lax.axis_size("x")
    )
    right = jnp.concatenate([dot(upd, half_of(p_value_out[0], core, 0)), direct_out], axis=1)
    below = dot(upd, spread_e).astype(BF16)
    count = lax.axis_size("y")
    for k in range(1, count):
        start = jnp.maximum(plane - k, 0) * 2 * rank
        item = lax.dynamic_slice_in_dim(below, start, 2 * rank, 1)
        right = right + send(item, [(i, i - k) for i in range(k, count)]).astype(F32)
    right = (right + swap(jnp.concatenate([right[tokens:], right[:tokens]], axis=0))).astype(BF16)
    left = jnp.concatenate([first_in, second_in], axis=1)
    parts = lax.all_to_all(doc_sums(left, right, slots, core, rank), XZ, 0, 0)
    total = jnp.sum(parts.astype(F32), axis=0)
    tables = total.reshape(rank, 2, rank).transpose(1, 0, 2)
    return tables.reshape(1, 2, 1, rank * rank)


def solution(mesh):
    grid = Mesh(mesh.devices.reshape(4, 4, 8, 2), ("y", "x", "z", "c"))
    placed = (
        P("y", DP, None),
        P(DP, None),
        P("y", DP, None),
        P("y", DP, None),
        P("y", None, None),
        P("y", None, None),
        P("y", None, None),
        P("y", None, None),
        P(DP),
        P(),
    )
    return jax.shard_map(
        body, mesh=grid, in_specs=placed, out_specs=P("y", None, DP, None), check_vma=False
    )
```

```python
import jax
import jax.numpy as jnp
from jax import lax
from jax.sharding import Mesh, PartitionSpec as P

XZ = ("x", "z")
DP = ("x", "z", "c")
SWAP = [(0, 1), (1, 0)]
BF16 = jnp.bfloat16
F32 = jnp.float32


def dot(left, right, left_dim=1):
    return lax.dot_general(
        left, right, (((left_dim,), (0,)), ((), ())), preferred_element_type=F32
    )


def send(value, pairs):
    return lax.ppermute(value, "y", pairs)


def swap(value):
    return lax.ppermute(value, "c", SWAP)


def half_of(value, core, axis=1):
    width = value.shape[axis] // 2
    return lax.dynamic_slice_in_dim(value, core * width, width, axis)


def ordered(mine, core):
    got = swap(mine)
    return jnp.concatenate([jnp.where(core == 0, mine, got), jnp.where(core == 0, got, mine)])


def from_above(value, steps):
    count = lax.axis_size("y")
    return send(value, [(i, i - steps) for i in range(steps, count)])


def along_x(items):
    count = lax.axis_size("x")
    moved = [
        lax.ppermute(items[k], "x", [(i, (i + k) % count) for i in range(count)])
        for k in range(1, count)
    ]
    return jnp.concatenate([items[0]] + moved, axis=0)


def both_cores(value):
    return jnp.concatenate([value, swap(value)], axis=0)


def grams(wv, right, plane, core):
    kv, columns = wv.shape[1], right.shape[1]
    width = kv // 2
    near, far = send(wv, [(2, 0), (3, 1), (1, 2)]), send(wv, [(3, 2)])
    close, wide = send(right, [(1, 0), (2, 1), (0, 2)]), send(right, [(1, 3)])
    right = jnp.where(plane == 3, wide, close)
    lefts = [jnp.where(plane == 3, wv, near), wv, far]
    got = swap(jnp.concatenate([half_of(item, 1 - core) for item in lefts], axis=1))
    mine = jnp.concatenate([half_of(item, core) for item in lefts], axis=1)
    left = jnp.concatenate([mine, got], axis=0)
    rows = both_cores(right)
    main = dot(left[:, :width], rows, 0)
    own = [dot(left[:, k * width : (k + 1) * width], rows[:, kv:], 0) for k in range(3)]
    own = jnp.concatenate(own + [jnp.zeros((width, columns - 3 * (columns - kv)), F32)], axis=1)
    parts = jnp.where(plane == 2, own, main).astype(BF16)
    ranks = lax.axis_size(XZ)
    shape = (ranks, width // ranks, columns)
    slices = lax.all_to_all(parts.reshape(shape), XZ, 0, 0)
    total = jnp.sum(slices.astype(F32), axis=0).astype(BF16)
    every = lax.all_to_all(jnp.broadcast_to(total[None], shape), XZ, 0, 0)
    return every.reshape(width, columns)


def solve(half, plane, core, kv):
    block = half.shape[1] - kv
    first = send(half[:, : 3 * block], [(2, 0)])
    near = send(half[:, kv:], [(0, 1), (1, 2)])
    far = send(half[:, kv:], [(3, 1)])
    g31 = send(half[:, :kv], [(3, 0)])
    g32 = send(half[:, :kv], [(1, 0)])
    one = ordered(jnp.where(plane == 0, first[:, :block], near), core)
    two = jnp.where(plane == 0, first[:, block : 2 * block], far).astype(F32)
    two = ordered((two + dot(half[:, :kv], one)).astype(BF16), core)
    three = first[:, 2 * block :].astype(F32) + dot(g31, one) + dot(g32, two)
    return one, two, ordered(three.astype(BF16), core)


def full_rows(own, core):
    count = lax.axis_size("z")
    mine = lax.all_to_all(jnp.broadcast_to(own[None], (count, *own.shape)), "z", 0, 0)
    got = swap(mine)
    both = jnp.stack([jnp.where(core == 0, mine, got), jnp.where(core == 0, got, mine)], axis=1)
    return both.reshape(-1, own.shape[1])


def doc_sums(left, right, slots, core, rank):
    owners = lax.axis_size(XZ)
    named = 2 * jnp.arange(owners, dtype=jnp.int32) + core
    onehot = (slots[:, None] == named[None, :]).astype(BF16)
    spread = (onehot[:, :, None] * left[:, None, :]).reshape(left.shape[0], owners * 2 * rank)
    table = dot(spread, right, 0).reshape(owners, 2 * rank, 2 * rank)
    lane = lax.broadcasted_iota(jnp.int32, (1, rank, 2 * rank), 2)
    return jnp.where(lane < rank, table[:, :rank], table[:, rank:]).astype(BF16)


def body(
    hidden, cotangent, w_value, w_out_t, p_in, p_value_out, p_value_in, p_out, segments, owner_slot
):
    plane, core = lax.axis_index("y"), lax.axis_index("c")
    device = lax.axis_index(DP)
    wv, wo, acts = w_value[0], w_out_t[0], hidden[0]
    rows, kv = wv.shape
    rank = p_in.shape[2]
    documents = owner_slot.shape[0]

    projected = dot(wv, p_value_in[0]).astype(BF16)
    projected = lax.all_gather(projected, DP, axis=0, tiled=True)

    out_rows = lax.dynamic_slice_in_dim(p_out[0], device * rows, rows, 0)
    ends = jnp.concatenate([dot(wo, p_value_out[0]).astype(BF16), out_rows], axis=1)
    half = grams(wv, jnp.concatenate([wo, ends], axis=1), plane, core)

    places, place = lax.axis_size("x"), lax.axis_index("x")
    quarter = cotangent.shape[1] // places
    items = [
        lax.dynamic_slice_in_dim(cotangent, ((place + k) % places) * quarter, quarter, 1)
        for k in range(places)
    ]
    cot = along_x(items)
    cot_got = swap(cot)
    match = segments[:, None] == jnp.arange(documents, dtype=jnp.int32)[None, :]
    slots = jnp.sum(jnp.where(match, owner_slot[None, :], 0), axis=1)
    known = [dot(acts, p_in[0]), dot(acts, projected), slots.astype(F32)[:, None]]
    known = along_x([jnp.concatenate(known, axis=1).astype(BF16)] * places)
    known = both_cores(known)
    left, slots = known[:, : 2 * rank], known[:, 2 * rank].astype(jnp.int32)

    spread = solve(half, plane, core, kv)
    own = ends.astype(F32)
    for k in range(3):
        own = own + dot(from_above(wo, k + 1), spread[k])
    table = full_rows(own.astype(BF16), core)
    right = jnp.concatenate([dot(cot, table), dot(cot_got, table)], axis=0).astype(BF16)
    parts = lax.all_to_all(doc_sums(left, right, slots, core, rank), XZ, 0, 0)
    total = jnp.sum(parts.astype(F32), axis=0)
    tables = total.reshape(rank, 2, rank).transpose(1, 0, 2)
    return tables.reshape(1, 2, 1, rank * rank)


def solution(mesh):
    grid = Mesh(mesh.devices.reshape(4, 4, 8, 2), ("y", "x", "z", "c"))
    placed = (
        P("y", DP, None),
        P(DP, None),
        P("y", DP, None),
        P("y", DP, None),
        P("y", None, None),
        P("y", None, None),
        P("y", None, None),
        P("y", None, None),
        P(DP),
        P(),
    )
    return jax.shard_map(
        body, mesh=grid, in_specs=placed, out_specs=P("y", None, DP, None), check_vma=False
    )
```

```python
import jax
import jax.numpy as jnp
from jax import lax
from jax.experimental import pallas as pl
from jax.experimental.pallas import tpu as pltpu
from jax.sharding import Mesh, PartitionSpec as P

XZ = ("x", "z")
DP = ("x", "z", "c")
SWAP = [(0, 1), (1, 0)]
BF16 = jnp.bfloat16
F32 = jnp.float32


def dot(left, right, left_dim=1):
    return lax.dot_general(
        left, right, (((left_dim,), (0,)), ((), ())), preferred_element_type=F32
    )


def send(value, pairs):
    return lax.ppermute(value, "y", pairs)


def swap(value):
    return lax.ppermute(value, "c", SWAP)


def half_of(value, core, axis=1):
    width = value.shape[axis] // 2
    return lax.dynamic_slice_in_dim(value, core * width, width, axis)


def ordered(mine, core):
    got = swap(mine)
    return jnp.concatenate([jnp.where(core == 0, mine, got), jnp.where(core == 0, got, mine)])


def quarter_of(value, place, count):
    width = value.shape[1] // count
    return lax.dynamic_slice_in_dim(value, (place % count) * width, width, 1)


def along_x(value, steps):
    count = lax.axis_size("x")
    return lax.ppermute(value, "x", [(i, (i - steps) % count) for i in range(count)])


def packed_rows(wo, wv, p_value_in):
    count, place = lax.axis_size("x"), lax.axis_index("x")
    maps = lax.dot_general(
        p_value_in, wv, (((0,), (1,)), ((), ())), preferred_element_type=F32
    ).astype(BF16)
    around = [maps] + [along_x(maps, k) for k in range(1, count)]
    pieces = []
    for p in range(count):
        steps = (p - place) % count
        item = around[0]
        for k in range(1, count):
            item = jnp.where(steps == k, around[k], item)
        pieces.append(item)
    return jnp.concatenate([wo, jnp.concatenate(pieces, axis=1)], axis=0)


def product_kernel(near, one, two, three, act_0, act_1, act_2, act_3, block, parts, value, parts_sum, value_sum):
    step, last = pl.program_id(0), pl.num_programs(0) - 1
    ranks, height, kv = block.shape
    rows = near.shape[1] // ranks
    tokens = near.shape[0]

    @pl.when(step == 0)
    def _():
        parts_sum[...] = jnp.zeros_like(parts_sum)
        value_sum[...] = jnp.zeros_like(value_sum)

    left = jnp.concatenate([near[...], one[...], two[...], three[...]], axis=0)
    for k in range(0, ranks, 2):
        weights = block[k : k + 2, :rows, :].reshape(2 * rows, kv)
        parts_sum[...] += jnp.dot(
            left[:, k * rows : (k + 2) * rows], weights, preferred_element_type=F32
        )
        for x, act in enumerate((act_0, act_1, act_2, act_3)):
            maps = jnp.concatenate(
                [block[k + i, rows:, x * rows : (x + 1) * rows] for i in range(2)], axis=1
            )
            value_sum[...] += lax.dot_general(
                act[:, k * rows : (k + 2) * rows],
                maps,
                (((1,), (1,)), ((), ())),
                preferred_element_type=F32,
            )

    @pl.when(step == last)
    def _():
        parts[...] = parts_sum[...].astype(BF16)
        value[...] = value_sum[...].astype(BF16)


def products(moved, act, full):
    tokens, quarter = moved[0].shape
    count, height, kv = full.shape
    rows = quarter // count
    rank = height - rows
    ranks = 4
    steps = count // ranks
    places = len(moved)
    token_spec = pl.BlockSpec((tokens, ranks * rows), lambda i: (0, i))
    act_specs = [
        pl.BlockSpec((tokens, ranks * rows), lambda i, x=x: (0, x * steps + i)) for x in range(places)
    ]
    return pl.pallas_call(
        product_kernel,
        grid=(steps,),
        in_specs=[token_spec] * places + act_specs + [
            pl.BlockSpec((ranks, height, kv), lambda i: (i, 0, 0))
        ],
        out_specs=[
            pl.BlockSpec((places * tokens, kv), lambda i: (0, 0)),
            pl.BlockSpec((tokens, rank), lambda i: (0, 0)),
        ],
        out_shape=[
            jax.ShapeDtypeStruct((places * tokens, kv), BF16),
            jax.ShapeDtypeStruct((tokens, rank), BF16),
        ],
        scratch_shapes=[
            pltpu.VMEM((places * tokens, kv), F32),
            pltpu.VMEM((tokens, rank), F32),
        ],
        compiler_params=pltpu.CompilerParams(
            dimension_semantics=("arbitrary",), vmem_limit_bytes=32 * 1024 * 1024
        ),
        cost_estimate=pl.CostEstimate(
            flops=2 * places * tokens * quarter * (kv + rank),
            bytes_accessed=2 * (full.size + act.size + 4 * moved[0].size),
            transcendentals=0,
        ),
    )(*moved, act, act, act, act, full)


def exchanged(items):
    return [items[0]] + [along_x(items[k], -k) for k in range(1, len(items))]


def together(value, others):
    value, *others = lax.optimization_barrier((value, *others))
    return value, others


def grams(wv, right, plane, core, first, second, work):
    kv, columns = wv.shape[1], right.shape[1]
    width = kv // 2
    near, far = send(wv, [(3, 0), (2, 1)]), send(wv, [(3, 1)])
    above, below = send(right, [(0, 1), (1, 2), (2, 3)]), send(right, [(1, 0)])
    right = jnp.where(plane == 0, below, above)
    lefts = [jnp.where(plane == 0, near, wv), near, far]
    got = swap(jnp.concatenate([half_of(item, 1 - core) for item in lefts], axis=1))
    mine = jnp.concatenate([half_of(item, core) for item in lefts], axis=1)
    left = jnp.concatenate([mine, got], axis=0)
    rows = jnp.concatenate([right, swap(right)], axis=0)
    main = dot(left[:, :width], rows, 0)
    own = [dot(left[:, k * width : (k + 1) * width], rows[:, kv:], 0) for k in range(3)]
    own = jnp.concatenate(own + [jnp.zeros((width, columns - 3 * (columns - kv)), F32)], axis=1)
    parts = jnp.where(plane == 1, own, main).astype(BF16)
    parts, first = together(parts, first)
    ranks = lax.axis_size(XZ)
    shape = (ranks, width // ranks, columns)
    slices = lax.all_to_all(parts.reshape(shape), XZ, 0, 0)
    total = jnp.sum(slices.astype(F32), axis=0).astype(BF16)
    total, second = together(total, second)
    every = lax.all_to_all(jnp.broadcast_to(total[None], shape), XZ, 0, 0)
    every, done = together(every, work(first, second))
    return every.reshape(width, columns), second, done


def solve(half, plane, core, kv, parts):
    block = half.shape[1] - kv
    above = send(half, [(1, 2), (2, 3)])
    wrap = send(half, [(0, 3)])
    twice = send(half[:, : 3 * block], [(1, 3)])
    first = jnp.where(plane == 1, half[:, : 3 * block], above[:, : 3 * block])
    first = jnp.where(plane == 3, twice, first)
    second = jnp.where(plane == 2, half, above)
    f01, f02, f03 = (first[:, k * block : (k + 1) * block] for k in range(3))
    g21, g31, g32 = second[:, :kv], wrap[:, :kv], half[:, :kv]
    f12, f13, f23 = second[:, kv:], wrap[:, kv:], half[:, kv:]
    known = ordered(jnp.concatenate([f01, f12], axis=1), core)
    back = [along_x(item, k + 1) for k, item in enumerate(parts)]
    f01_all, f12_all = known[:, :block], known[:, block:]
    e02 = (f02.astype(F32) + dot(g21, f01_all)).astype(BF16)
    e02_all, back = together(ordered(e02, core), back)
    e13 = (f13.astype(F32) + dot(g32, f12_all)).astype(BF16)
    e03 = (f03.astype(F32) + dot(g31, f01_all) + dot(g32, e02_all)).astype(BF16)
    zero = jnp.zeros_like(f01)
    columns = (
        jnp.where(plane == 1, f01, jnp.where(plane == 2, e02, e03)),
        jnp.where(plane == 2, f12, jnp.where(plane == 3, e13, zero)),
        jnp.where(plane == 3, f23, zero),
    )
    return jnp.concatenate(columns, axis=1), back


def doc_sums(left, right, slots, core, rank):
    owners = lax.axis_size(XZ)
    named = 2 * jnp.arange(owners, dtype=jnp.int32) + core
    onehot = (slots[:, None] == named[None, :]).astype(BF16)
    spread = (onehot[:, :, None] * left[:, None, :]).reshape(left.shape[0], owners * 2 * rank)
    table = dot(spread, right, 0).reshape(owners, 2 * rank, 2 * rank)
    lane = lax.broadcasted_iota(jnp.int32, (1, rank, 2 * rank), 2)
    return jnp.where(lane < rank, table[:, :rank], table[:, rank:]).astype(BF16)


def body(
    hidden, cotangent, w_value, w_out_t, p_in, p_value_out, p_value_in, p_out, segments, owner_slot
):
    plane, core = lax.axis_index("y"), lax.axis_index("c")
    device = lax.axis_index(DP)
    wv, wo, acts = w_value[0], w_out_t[0], hidden[0]
    rows, kv = wv.shape
    rank = p_in.shape[2]
    documents = owner_slot.shape[0]

    places, place = lax.axis_size("x"), lax.axis_index("x")
    items = [quarter_of(cotangent, place + k, places) for k in range(places)]
    wv, items = together(wv, items)
    moved = exchanged(items)
    mixed = packed_rows(wo, wv, p_value_in[0])
    wv, (wo, mixed) = together(wv, [wo, mixed])
    full = lax.all_gather(mixed[None], ("z", "c"), axis=0, tiled=True)

    match = segments[:, None] == jnp.arange(documents, dtype=jnp.int32)[None, :]
    slots = jnp.sum(jnp.where(match, owner_slot[None, :], 0), axis=1)
    first_in = dot(acts, p_in[0]).astype(BF16)
    direct_out = dot(cotangent, p_out[0])
    out_rows = lax.dynamic_slice_in_dim(p_out[0], device * rows, rows, 0)
    right_rows = jnp.concatenate([wo, dot(wo, p_value_out[0]).astype(BF16), out_rows], axis=1)
    early = [first_in, direct_out, jnp.concatenate([slots, swap(slots)]), moved[2]]

    def work(near, early):
        tokens = acts.shape[0]
        parts, value = products([near[0], near[1], early[3], near[2]], acts, full)
        return [value] + [parts[k * tokens : (k + 1) * tokens] for k in range(places)]

    half, early, done = grams(
        wv, right_rows, plane, core, [moved[0], moved[1], moved[3]], early, work
    )
    first_in, direct_out, slots, far = early
    second_in, upd = done[0], done[1]
    spread_e, back = solve(half, plane, core, kv, done[2:])
    spread_e = ordered(spread_e, core)
    upd = (upd.astype(F32) + sum(item.astype(F32) for item in back)).astype(BF16)
    right = jnp.concatenate([dot(upd, p_value_out[0]), direct_out], axis=1)
    below = dot(upd, spread_e).astype(BF16)
    count = lax.axis_size("y")
    for k in range(1, count):
        start = jnp.maximum(plane - k, 0) * 2 * rank
        item = lax.dynamic_slice_in_dim(below, start, 2 * rank, 1)
        right = right + send(item, [(i, i - k) for i in range(k, count)]).astype(F32)
    packed = jnp.concatenate([first_in, second_in, right.astype(BF16)], axis=1)
    packed = jnp.concatenate([packed, swap(packed)], axis=0)
    left, right = packed[:, : 2 * rank], packed[:, 2 * rank :]
    parts = lax.all_to_all(doc_sums(left, right, slots, core, rank), XZ, 0, 0)
    total = jnp.sum(parts.astype(F32), axis=0)
    tables = total.reshape(rank, 2, rank).transpose(1, 0, 2)
    return tables.reshape(1, 2, 1, rank * rank)


def solution(mesh):
    grid = Mesh(mesh.devices.reshape(4, 4, 8, 2), ("y", "x", "z", "c"))
    placed = (
        P("y", DP, None),
        P(DP, None),
        P("y", DP, None),
        P("y", DP, None),
        P("y", None, None),
        P("y", None, None),
        P("y", None, None),
        P("y", None, None),
        P(DP),
        P(),
    )
    return jax.shard_map(
        body, mesh=grid, in_specs=placed, out_specs=P("y", None, DP, None), check_vma=False
    )
```

```python
import jax
import jax.numpy as jnp
from jax import lax
from jax.experimental import pallas as pl
from jax.experimental.pallas import tpu as pltpu
from jax.sharding import Mesh, PartitionSpec as P

XZ = ("x", "z")
DP = ("x", "z", "c")
SWAP = [(0, 1), (1, 0)]
BF16 = jnp.bfloat16
F32 = jnp.float32


def dot(left, right, left_dim=1):
    return lax.dot_general(
        left, right, (((left_dim,), (0,)), ((), ())), preferred_element_type=F32
    )


def send(value, pairs):
    return lax.ppermute(value, "y", pairs)


def swap(value):
    return lax.ppermute(value, "c", SWAP)


def half_of(value, core, axis=1):
    width = value.shape[axis] // 2
    return lax.dynamic_slice_in_dim(value, core * width, width, axis)


def ordered(mine, core):
    got = swap(mine)
    return jnp.concatenate([jnp.where(core == 0, mine, got), jnp.where(core == 0, got, mine)])


def quarter_of(value, place, count):
    width = value.shape[1] // count
    return lax.dynamic_slice_in_dim(value, (place % count) * width, width, 1)


def along_x(value, steps):
    count = lax.axis_size("x")
    return lax.ppermute(value, "x", [(i, (i - steps) % count) for i in range(count)])


def packed_rows(wo, wv, p_value_in):
    count, place = lax.axis_size("x"), lax.axis_index("x")
    maps = lax.dot_general(
        p_value_in, wv, (((0,), (1,)), ((), ())), preferred_element_type=F32
    ).astype(BF16)
    around = [maps] + [along_x(maps, k) for k in range(1, count)]
    pieces = []
    for p in range(count):
        steps = (p - place) % count
        item = around[0]
        for k in range(1, count):
            item = jnp.where(steps == k, around[k], item)
        pieces.append(item)
    return jnp.concatenate([wo, jnp.concatenate(pieces, axis=1)], axis=0)


def product_kernel(near, one, two, three, act_0, act_1, act_2, act_3, block, parts, value, parts_sum, value_sum):
    step, last = pl.program_id(0), pl.num_programs(0) - 1
    ranks, height, kv = block.shape
    rows = near.shape[1] // ranks
    tokens = near.shape[0]

    @pl.when(step == 0)
    def _():
        parts_sum[...] = jnp.zeros_like(parts_sum)
        value_sum[...] = jnp.zeros_like(value_sum)

    left = jnp.concatenate([near[...], one[...], two[...], three[...]], axis=0)
    for k in range(0, ranks, 2):
        weights = block[k : k + 2, :rows, :].reshape(2 * rows, kv)
        parts_sum[...] += jnp.dot(
            left[:, k * rows : (k + 2) * rows], weights, preferred_element_type=F32
        )
        for x, act in enumerate((act_0, act_1, act_2, act_3)):
            maps = jnp.concatenate(
                [block[k + i, rows:, x * rows : (x + 1) * rows] for i in range(2)], axis=1
            )
            value_sum[...] += lax.dot_general(
                act[:, k * rows : (k + 2) * rows],
                maps,
                (((1,), (1,)), ((), ())),
                preferred_element_type=F32,
            )

    @pl.when(step == last)
    def _():
        parts[...] = parts_sum[...].astype(BF16)
        value[...] = value_sum[...].astype(BF16)


def products(moved, act, full):
    tokens, quarter = moved[0].shape
    count, height, kv = full.shape
    rows = quarter // count
    rank = height - rows
    ranks = 4
    steps = count // ranks
    places = len(moved)
    token_spec = pl.BlockSpec((tokens, ranks * rows), lambda i: (0, i))
    act_specs = [
        pl.BlockSpec((tokens, ranks * rows), lambda i, x=x: (0, x * steps + i)) for x in range(places)
    ]
    return pl.pallas_call(
        product_kernel,
        grid=(steps,),
        in_specs=[token_spec] * places + act_specs + [
            pl.BlockSpec((ranks, height, kv), lambda i: (i, 0, 0))
        ],
        out_specs=[
            pl.BlockSpec((places * tokens, kv), lambda i: (0, 0)),
            pl.BlockSpec((tokens, rank), lambda i: (0, 0)),
        ],
        out_shape=[
            jax.ShapeDtypeStruct((places * tokens, kv), BF16),
            jax.ShapeDtypeStruct((tokens, rank), BF16),
        ],
        scratch_shapes=[
            pltpu.VMEM((places * tokens, kv), F32),
            pltpu.VMEM((tokens, rank), F32),
        ],
        compiler_params=pltpu.CompilerParams(
            dimension_semantics=("arbitrary",), vmem_limit_bytes=32 * 1024 * 1024
        ),
        cost_estimate=pl.CostEstimate(
            flops=2 * places * tokens * quarter * (kv + rank),
            bytes_accessed=2 * (full.size + act.size + 4 * moved[0].size),
            transcendentals=0,
        ),
    )(*moved, act, act, act, act, full)


def exchanged(items):
    return [items[0]] + [along_x(items[k], -k) for k in range(1, len(items))]


def together(value, others):
    value, *others = lax.optimization_barrier((value, *others))
    return value, others


def grams(wv, right, plane, core, first, second, work):
    kv, columns = wv.shape[1], right.shape[1]
    width = kv // 2
    near, far = send(wv, [(3, 0), (2, 1)]), send(wv, [(3, 1)])
    above, below = send(right, [(0, 1), (1, 2), (2, 3)]), send(right, [(1, 0)])
    right = jnp.where(plane == 0, below, above)
    lefts = [jnp.where(plane == 0, near, wv), near, far]
    got = swap(jnp.concatenate([half_of(item, 1 - core) for item in lefts], axis=1))
    mine = jnp.concatenate([half_of(item, core) for item in lefts], axis=1)
    left = jnp.concatenate([mine, got], axis=0)
    rows = jnp.concatenate([right, swap(right)], axis=0)
    main = dot(left[:, :width], rows, 0)
    own = [dot(left[:, k * width : (k + 1) * width], rows[:, kv:], 0) for k in range(3)]
    own = jnp.concatenate(own + [jnp.zeros((width, columns - 3 * (columns - kv)), F32)], axis=1)
    parts = jnp.where(plane == 1, own, main).astype(BF16)
    parts, first = together(parts, first)
    ranks = lax.axis_size(XZ)
    shape = (ranks, width // ranks, columns)
    slices = lax.all_to_all(parts.reshape(shape), XZ, 0, 0)
    total = jnp.sum(slices.astype(F32), axis=0).astype(BF16)
    total, second = together(total, second)
    every = lax.all_to_all(jnp.broadcast_to(total[None], shape), XZ, 0, 0)
    every, done = together(every, work(first, second))
    return every.reshape(width, columns), second, done


def solve(half, plane, core, kv, parts):
    block = half.shape[1] - kv
    above = send(half, [(1, 2), (2, 3)])
    wrap = send(half, [(0, 3)])
    twice = send(half[:, : 3 * block], [(1, 3)])
    first = jnp.where(plane == 1, half[:, : 3 * block], above[:, : 3 * block])
    first = jnp.where(plane == 3, twice, first)
    second = jnp.where(plane == 2, half, above)
    f01, f02, f03 = (first[:, k * block : (k + 1) * block] for k in range(3))
    g21, g31, g32 = second[:, :kv], wrap[:, :kv], half[:, :kv]
    f12, f13, f23 = second[:, kv:], wrap[:, kv:], half[:, kv:]
    known = ordered(jnp.concatenate([f01, f12], axis=1), core)
    back = [along_x(item, k + 1) for k, item in enumerate(parts)]
    f01_all, f12_all = known[:, :block], known[:, block:]
    e02 = (f02.astype(F32) + dot(g21, f01_all)).astype(BF16)
    e02_all, back = together(ordered(e02, core), back)
    e13 = (f13.astype(F32) + dot(g32, f12_all)).astype(BF16)
    e03 = (f03.astype(F32) + dot(g31, f01_all) + dot(g32, e02_all)).astype(BF16)
    zero = jnp.zeros_like(f01)
    columns = (
        jnp.where(plane == 0, zero, jnp.where(plane == 1, f01, jnp.where(plane == 2, e02, e03))),
        jnp.where(plane == 2, f12, jnp.where(plane == 3, e13, zero)),
        jnp.where(plane == 3, f23, zero),
    )
    return jnp.concatenate(columns, axis=1), back


def doc_sums(left, right, slots, core, rank):
    owners = lax.axis_size(XZ)
    named = 2 * jnp.arange(owners, dtype=jnp.int32) + core
    onehot = (slots[:, None] == named[None, :]).astype(BF16)
    spread = (onehot[:, :, None] * left[:, None, :]).reshape(left.shape[0], owners * 2 * rank)
    table = dot(spread, right, 0).reshape(owners, 2 * rank, 2 * rank)
    lane = lax.broadcasted_iota(jnp.int32, (1, rank, 2 * rank), 2)
    return jnp.where(lane < rank, table[:, :rank], table[:, rank:]).astype(BF16)


def body(
    hidden, cotangent, w_value, w_out_t, p_in, p_value_out, p_value_in, p_out, segments, owner_slot
):
    plane, core = lax.axis_index("y"), lax.axis_index("c")
    device = lax.axis_index(DP)
    wv, wo, acts = w_value[0], w_out_t[0], hidden[0]
    rows, kv = wv.shape
    rank = p_in.shape[2]
    documents = owner_slot.shape[0]

    places, place = lax.axis_size("x"), lax.axis_index("x")
    items = [quarter_of(cotangent, place + k, places) for k in range(places)]
    wv, items = together(wv, items)
    moved = exchanged(items)
    mixed = packed_rows(wo, wv, p_value_in[0])
    wv, (wo, mixed) = together(wv, [wo, mixed])
    full = lax.all_gather(mixed[None], ("z", "c"), axis=0, tiled=True)

    match = segments[:, None] == jnp.arange(documents, dtype=jnp.int32)[None, :]
    slots = jnp.sum(jnp.where(match, owner_slot[None, :], 0), axis=1)
    first_in = dot(acts, p_in[0]).astype(BF16)
    direct_out = dot(cotangent, p_out[0])
    out_rows = lax.dynamic_slice_in_dim(p_out[0], device * rows, rows, 0)
    right_rows = jnp.concatenate([wo, dot(wo, p_value_out[0]).astype(BF16), out_rows], axis=1)
    early = [first_in, direct_out, jnp.concatenate([slots, swap(slots)]), moved[2]]

    def work(near, early):
        tokens = acts.shape[0]
        parts, value = products([near[0], near[1], early[3], near[2]], acts, full)
        return [value] + [parts[k * tokens : (k + 1) * tokens] for k in range(places)]

    half, early, done = grams(
        wv, right_rows, plane, core, [moved[0], moved[1], moved[3]], early, work
    )
    first_in, direct_out, slots, far = early
    second_in, upd = done[0], done[1]
    spread_e, back = solve(half, plane, core, kv, done[2:])
    spread_e = ordered(spread_e, core)
    upd = (upd.astype(F32) + sum(item.astype(F32) for item in back)).astype(BF16)
    right = jnp.concatenate([dot(upd, p_value_out[0]), direct_out], axis=1)
    count = lax.axis_size("y")
    below = [dot(upd, spread_e[:, 2 * k * rank : 2 * (k + 1) * rank]).astype(BF16) for k in range(count - 1)]
    below = jnp.stack(below + [jnp.zeros_like(below[0])])
    right = right + jnp.sum(lax.all_to_all(below, "y", 0, 0).astype(F32), axis=0)
    packed = jnp.concatenate([first_in, second_in, right.astype(BF16)], axis=1)
    packed = jnp.concatenate([packed, swap(packed)], axis=0)
    left, right = packed[:, : 2 * rank], packed[:, 2 * rank :]
    parts = lax.all_to_all(doc_sums(left, right, slots, core, rank), XZ, 0, 0)
    total = jnp.sum(parts.astype(F32), axis=0)
    tables = total.reshape(rank, 2, rank).transpose(1, 0, 2)
    return tables.reshape(1, 2, 1, rank * rank)


def solution(mesh):
    grid = Mesh(mesh.devices.reshape(4, 4, 8, 2), ("y", "x", "z", "c"))
    placed = (
        P("y", DP, None),
        P(DP, None),
        P("y", DP, None),
        P("y", DP, None),
        P("y", None, None),
        P("y", None, None),
        P("y", None, None),
        P("y", None, None),
        P(DP),
        P(),
    )
    return jax.shard_map(
        body, mesh=grid, in_specs=placed, out_specs=P("y", None, DP, None), check_vma=False
    )
```

```python
import jax
import jax.numpy as jnp
from jax import lax
from jax.experimental import pallas as pl
from jax.experimental.pallas import tpu as pltpu
from jax.sharding import Mesh, PartitionSpec as P

XZ = ("x", "z")
DP = ("x", "z", "c")
SWAP = [(0, 1), (1, 0)]
BF16 = jnp.bfloat16
F32 = jnp.float32


def dot(left, right, left_dim=1):
    return lax.dot_general(
        left, right, (((left_dim,), (0,)), ((), ())), preferred_element_type=F32
    )


def send(value, pairs):
    return lax.ppermute(value, "y", pairs)


def swap(value):
    return lax.ppermute(value, "c", SWAP)


def half_of(value, core, axis=1):
    width = value.shape[axis] // 2
    return lax.dynamic_slice_in_dim(value, core * width, width, axis)


def ordered(mine, core):
    got = swap(mine)
    return jnp.concatenate([jnp.where(core == 0, mine, got), jnp.where(core == 0, got, mine)])


def quarter_of(value, place, count):
    width = value.shape[1] // count
    return lax.dynamic_slice_in_dim(value, (place % count) * width, width, 1)


def along_x(value, steps):
    count = lax.axis_size("x")
    return lax.ppermute(value, "x", [(i, (i - steps) % count) for i in range(count)])


def packed_rows(wo, wv, p_value_in):
    count, place = lax.axis_size("x"), lax.axis_index("x")
    maps = lax.dot_general(
        p_value_in, wv, (((0,), (1,)), ((), ())), preferred_element_type=F32
    ).astype(BF16)
    around = [maps] + [along_x(maps, k) for k in range(1, count)]
    pieces = []
    for p in range(count):
        steps = (p - place) % count
        item = around[0]
        for k in range(1, count):
            item = jnp.where(steps == k, around[k], item)
        pieces.append(item)
    return jnp.concatenate([wo, jnp.concatenate(pieces, axis=1)], axis=0)


def product_kernel(near, one, two, three, act_0, act_1, act_2, act_3, block, parts, value, parts_sum, value_sum):
    step, last = pl.program_id(0), pl.num_programs(0) - 1
    ranks, height, kv = block.shape
    rows = near.shape[1] // ranks
    tokens = near.shape[0]

    @pl.when(step == 0)
    def _():
        parts_sum[...] = jnp.zeros_like(parts_sum)
        value_sum[...] = jnp.zeros_like(value_sum)

    left = jnp.concatenate([near[...], one[...], two[...], three[...]], axis=0)
    for k in range(0, ranks, 2):
        weights = block[k : k + 2, :rows, :].reshape(2 * rows, kv)
        parts_sum[...] += jnp.dot(
            left[:, k * rows : (k + 2) * rows], weights, preferred_element_type=F32
        )
        for x, act in enumerate((act_0, act_1, act_2, act_3)):
            maps = jnp.concatenate(
                [block[k + i, rows:, x * rows : (x + 1) * rows] for i in range(2)], axis=1
            )
            value_sum[...] += lax.dot_general(
                act[:, k * rows : (k + 2) * rows],
                maps,
                (((1,), (1,)), ((), ())),
                preferred_element_type=F32,
            )

    @pl.when(step == last)
    def _():
        parts[...] = parts_sum[...].astype(BF16)
        value[...] = value_sum[...].astype(BF16)


def products(moved, act, full):
    tokens, quarter = moved[0].shape
    count, height, kv = full.shape
    rows = quarter // count
    rank = height - rows
    ranks = 4
    steps = count // ranks
    places = len(moved)
    token_spec = pl.BlockSpec((tokens, ranks * rows), lambda i: (0, i))
    act_specs = [
        pl.BlockSpec((tokens, ranks * rows), lambda i, x=x: (0, x * steps + i)) for x in range(places)
    ]
    return pl.pallas_call(
        product_kernel,
        grid=(steps,),
        in_specs=[token_spec] * places + act_specs + [
            pl.BlockSpec((ranks, height, kv), lambda i: (i, 0, 0))
        ],
        out_specs=[
            pl.BlockSpec((places * tokens, kv), lambda i: (0, 0)),
            pl.BlockSpec((tokens, rank), lambda i: (0, 0)),
        ],
        out_shape=[
            jax.ShapeDtypeStruct((places * tokens, kv), BF16),
            jax.ShapeDtypeStruct((tokens, rank), BF16),
        ],
        scratch_shapes=[
            pltpu.VMEM((places * tokens, kv), F32),
            pltpu.VMEM((tokens, rank), F32),
        ],
        compiler_params=pltpu.CompilerParams(
            dimension_semantics=("arbitrary",), vmem_limit_bytes=32 * 1024 * 1024
        ),
        cost_estimate=pl.CostEstimate(
            flops=2 * places * tokens * quarter * (kv + rank),
            bytes_accessed=2 * (full.size + act.size + 4 * moved[0].size),
            transcendentals=0,
        ),
    )(*moved, act, act, act, act, full)


def exchanged(items):
    return [along_x(item, -k - 1) for k, item in enumerate(items)]


def together(value, others):
    value, *others = lax.optimization_barrier((value, *others))
    return value, others


def grams(wv, right, plane, core, first, second, work):
    kv, columns = wv.shape[1], right.shape[1]
    width = kv // 2
    near, far = send(wv, [(3, 0), (2, 1)]), send(wv, [(3, 1)])
    above, below = send(right, [(0, 1), (1, 2), (2, 3)]), send(right, [(1, 0)])
    right = jnp.where(plane == 0, below, above)
    lefts = [jnp.where(plane == 0, near, wv), near, far]
    got = swap(jnp.concatenate([half_of(item, 1 - core) for item in lefts], axis=1))
    mine = jnp.concatenate([half_of(item, core) for item in lefts], axis=1)
    left = jnp.concatenate([mine, got], axis=0)
    rows = jnp.concatenate([right, swap(right)], axis=0)
    main = dot(left[:, :width], rows, 0)
    own = [dot(left[:, k * width : (k + 1) * width], rows[:, kv:], 0) for k in range(3)]
    own = jnp.concatenate(own + [jnp.zeros((width, columns - 3 * (columns - kv)), F32)], axis=1)
    parts = jnp.where(plane == 1, own, main).astype(BF16)
    parts, first = together(parts, first)
    ranks = lax.axis_size(XZ)
    shape = (ranks, width // ranks, columns)
    slices = lax.all_to_all(parts.reshape(shape), XZ, 0, 0)
    total = jnp.sum(slices.astype(F32), axis=0).astype(BF16)
    total, second = together(total, second)
    every = lax.all_to_all(jnp.broadcast_to(total[None], shape), XZ, 0, 0)
    every, done = together(every, work(first, second))
    return every.reshape(width, columns), second, done


def solve(half, plane, core, kv, parts):
    block = half.shape[1] - kv
    above = send(half, [(1, 2), (2, 3)])
    wrap = send(half, [(0, 3)])
    twice = send(half[:, : 3 * block], [(1, 3)])
    first = jnp.where(plane == 1, half[:, : 3 * block], above[:, : 3 * block])
    first = jnp.where(plane == 3, twice, first)
    second = jnp.where(plane == 2, half, above)
    f01, f02, f03 = (first[:, k * block : (k + 1) * block] for k in range(3))
    g21, g31, g32 = second[:, :kv], wrap[:, :kv], half[:, :kv]
    f12, f13, f23 = second[:, kv:], wrap[:, kv:], half[:, kv:]
    known = ordered(jnp.concatenate([f01, f12], axis=1), core)
    back = [along_x(item, k + 1) for k, item in enumerate(parts)]
    f01_all, f12_all = known[:, :block], known[:, block:]
    e02 = (f02.astype(F32) + dot(g21, f01_all)).astype(BF16)
    e02_all, back = together(ordered(e02, core), back)
    e13 = (f13.astype(F32) + dot(g32, f12_all)).astype(BF16)
    e03 = (f03.astype(F32) + dot(g31, f01_all) + dot(g32, e02_all)).astype(BF16)
    zero = jnp.zeros_like(f01)
    columns = (
        jnp.where(plane == 0, zero, jnp.where(plane == 1, f01, jnp.where(plane == 2, e02, e03))),
        jnp.where(plane == 2, f12, jnp.where(plane == 3, e13, zero)),
        jnp.where(plane == 3, f23, zero),
    )
    return jnp.concatenate(columns, axis=1), back


def doc_sums(left, right, slots, core, rank):
    owners = lax.axis_size(XZ)
    named = 2 * jnp.arange(owners, dtype=jnp.int32) + core
    onehot = (slots[:, None] == named[None, :]).astype(BF16)
    spread = (onehot[:, :, None] * left[:, None, :]).reshape(left.shape[0], owners * 2 * rank)
    table = dot(spread, right, 0).reshape(owners, 2 * rank, 2 * rank)
    lane = lax.broadcasted_iota(jnp.int32, (1, rank, 2 * rank), 2)
    return jnp.where(lane < rank, table[:, :rank], table[:, rank:]).astype(BF16)


def body(
    hidden, cotangent, w_value, w_out_t, p_in, p_value_out, p_value_in, p_out, segments, owner_slot
):
    plane, core = lax.axis_index("y"), lax.axis_index("c")
    device = lax.axis_index(DP)
    wv, wo, acts = w_value[0], w_out_t[0], hidden[0]
    rows, kv = wv.shape
    rank = p_in.shape[2]
    documents = owner_slot.shape[0]

    places, place = lax.axis_size("x"), lax.axis_index("x")
    items = [quarter_of(cotangent, place + k, places) for k in range(1, places)]
    wv, items = together(wv, items)
    moved = exchanged(items)
    mixed = packed_rows(wo, wv, p_value_in[0])
    wv, (wo, mixed) = together(wv, [wo, mixed])
    full = lax.all_gather(mixed[None], ("z", "c"), axis=0, tiled=True)

    match = segments[:, None] == jnp.arange(documents, dtype=jnp.int32)[None, :]
    slots = jnp.sum(jnp.where(match, owner_slot[None, :], 0), axis=1)
    first_in = dot(acts, p_in[0]).astype(BF16)
    direct_out = dot(cotangent, p_out[0])
    out_rows = lax.dynamic_slice_in_dim(p_out[0], device * rows, rows, 0)
    right_rows = jnp.concatenate([wo, dot(wo, p_value_out[0]).astype(BF16), out_rows], axis=1)
    early = [first_in, direct_out, jnp.concatenate([slots, swap(slots)]), moved[1]]

    def work(near, early):
        tokens = acts.shape[0]
        parts, value = products([quarter_of(near[0], place, places), near[1], early[3], near[2]], acts, full)
        return [value] + [parts[k * tokens : (k + 1) * tokens] for k in range(places)]

    half, early, done = grams(
        wv, right_rows, plane, core, [cotangent, moved[0], moved[2]], early, work
    )
    first_in, direct_out, slots, far = early
    second_in, upd = done[0], done[1]
    spread_e, back = solve(half, plane, core, kv, done[2:])
    spread_e = ordered(spread_e, core)
    upd = (upd.astype(F32) + sum(item.astype(F32) for item in back)).astype(BF16)
    right = jnp.concatenate([dot(upd, p_value_out[0]), direct_out], axis=1)
    count = lax.axis_size("y")
    below = [dot(upd, spread_e[:, 2 * k * rank : 2 * (k + 1) * rank]).astype(BF16) for k in range(count - 1)]
    below = jnp.stack(below + [jnp.zeros_like(below[0])])
    right = right + jnp.sum(lax.all_to_all(below, "y", 0, 0).astype(F32), axis=0)
    packed = jnp.concatenate([first_in, second_in, right.astype(BF16)], axis=1)
    packed = jnp.concatenate([packed, swap(packed)], axis=0)
    left, right = packed[:, : 2 * rank], packed[:, 2 * rank :]
    parts = lax.all_to_all(doc_sums(left, right, slots, core, rank), XZ, 0, 0)
    total = jnp.sum(parts.astype(F32), axis=0)
    tables = total.reshape(rank, 2, rank).transpose(1, 0, 2)
    return tables.reshape(1, 2, 1, rank * rank)


def solution(mesh):
    grid = Mesh(mesh.devices.reshape(4, 4, 8, 2), ("y", "x", "z", "c"))
    placed = (
        P("y", DP, None),
        P(DP, None),
        P("y", DP, None),
        P("y", DP, None),
        P("y", None, None),
        P("y", None, None),
        P("y", None, None),
        P("y", None, None),
        P(DP),
        P(),
    )
    return jax.shard_map(
        body, mesh=grid, in_specs=placed, out_specs=P("y", None, DP, None), check_vma=False
    )
```
